256 devices in a mesh: chrom: 4 (over z_hi), tile: 32 (over y, x, z_lo), var: 2 (over core).
Axes of the slice: x: 4, y: 4, z: 8 (z_hi: 4, z_lo: 2; z = z_hi * 2 + z_lo), core: 2. Of those that a mesh axis runs over, the one named last changes fastest.
Arguments:
- row_geno: int32 [12288, 2048], P('tile', ('chrom', 'var')), may hold values from 0 to 2, as said below
- col_geno: int32 [4096, 2048], P(('tile', 'var'), 'chrom'), may hold values from 0 to 2, as said below
- allele_freq: float32 [2048], P(('chrom', 'var')), may hold values from 0.05000305 to 0.5, as said below
- snp_counts: int32 [8], replicated, may hold values from 1 to 512, 2048 in all
- group_of: int32 [8], replicated, may hold values from 0 to 3, as said below
- pair_mask: int32 [8, 8], replicated, may hold values 0 or 1
- probes: bfloat16 [4096, 128], P(('tile', 'var')), may hold values from -6 to 6
Outputs:
- kernel_out: bfloat16 [4, 12288, 128], P('chrom', 'tile')
The draws below stay inside these ranges and needn't reach their ends.
Inputs may be any that keep to these rules, and one draw needn't show every extreme that they name: `group_of`: every group holds at most 4 chromosomes, and some group holds exactly 4. `pair_mask`: the diagonal is not used. `snp_counts`: the counts sum to 2048; the largest is 512. `allele_freq`: multiples of 1 / 65536. `row_geno`: each code is the number of base alleles among two drawn independently, each with the probability allele_freq of its variant. `col_geno`: each code is the number of base alleles among two drawn independently, each with the probability allele_freq of its variant.
All inputs are finite; a program needn't handle non-finite values.
Results may differ from the reference program's by a relative error of at most 0.019.
Values may be sent and summed in bfloat16 or wider, within the bound.
No kernel may reach another device: no remote copies, remote signals or barrier semaphores. Data moves between devices by JAX's collectives and lax.ppermute only.
A program may use at most 64 MiB of HBM per device.

```python
import math
import jax
import jax.numpy as jnp
import numpy as np
from jax import lax

VARIANTS = 2048
PROBES = 128
MOST_CHR = 4
ROW_DEV = 384
GROUPS = 4
CHROMS = 8
MOST_SNP = 512
ROWS = 12288
COLS = 4096


def draw_group_of(key, part):
    folded = jax.random.fold_in(key, 11)
    first_key, second_key, third_key = jax.random.split(folded, 3)
    fullest = jax.random.randint(first_key, (), 0, GROUPS, dtype=jnp.int32)
    others = jax.random.permutation(second_key, (GROUPS - 1) * MOST_CHR).astype(jnp.int32)
    remain = (fullest + 1 + others[:CHROMS - MOST_CHR] // MOST_CHR) % GROUPS
    labels = jnp.concatenate([jnp.full((MOST_CHR,), fullest, jnp.int32), remain.astype(jnp.int32)])
    order = jax.random.permutation(third_key, CHROMS)
    return labels[order].astype(jnp.int32)


def allele_levels(key):
    folded = jax.random.fold_in(key, 23)
    level_key, low_key, high_key = jax.random.split(folded, 3)
    levels = jax.random.randint(level_key, (VARIANTS,), 3277, 32769, dtype=jnp.int32)
    low_at = jax.random.randint(low_key, (), 0, VARIANTS, dtype=jnp.int32)
    high_at = (low_at + 1 + jax.random.randint(high_key, (), 0, VARIANTS - 1, dtype=jnp.int32)) % VARIANTS
    position = jnp.arange(VARIANTS, dtype=jnp.int32)
    levels = jnp.where(position == low_at, jnp.int32(3277), levels)
    levels = jnp.where(position == high_at, jnp.int32(32768), levels)
    return levels.astype(jnp.int32)


def allele_pairs(key, stream, row_count):
    levels = allele_levels(key)
    folded = jax.random.fold_in(key, stream)
    first_key, second_key = jax.random.split(folded, 2)
    first_draw = jax.random.randint(first_key, (row_count, VARIANTS), 0, 65536, dtype=jnp.int32)
    second_draw = jax.random.randint(second_key, (row_count, VARIANTS), 0, 65536, dtype=jnp.int32)
    first_allele = (first_draw < levels[None, :]).astype(jnp.int32)
    second_allele = (second_draw < levels[None, :]).astype(jnp.int32)
    return (first_allele + second_allele).astype(jnp.int32)


def draw_allele_freq(key, part):
    return (allele_levels(key).astype(jnp.float32) / 65536.0).astype(jnp.float32)


def draw_row_geno(key, part):
    return allele_pairs(key, 31, ROWS)


def draw_col_geno(key, part):
    return allele_pairs(key, 37, COLS)


def place_ends(drawn, own_key, least, high):
    longest = drawn.shape.index(max(drawn.shape))
    spots = []
    for shift in (0, 1):
        where = [jax.random.randint(jax.random.fold_in(own_key, axis), (), 0, length) for axis, length in enumerate(drawn.shape)]
        where[longest] = (where[longest] + shift) % drawn.shape[longest]
        spots.append(tuple(where))
    return drawn.at[spots[0]].set(least).at[spots[1]].set(high)


def block_scale(own_key, dims, pieces, smallest, top_value):
    loudness, own = 1.0, jax.random.fold_in(own_key, 6)
    for axis_at, shards_of in pieces:
        draws = jnp.exp(jax.random.uniform(jax.random.fold_in(own, axis_at), (shards_of,), jnp.float32, smallest / len(pieces), top_value / len(pieces)))
        loudness = loudness * jnp.repeat(draws, dims[axis_at] // shards_of).reshape([-1 if axis == axis_at else 1 for axis in range(len(dims))])
    return loudness


def split_up(amount, total, bound, skew):
    weights = [(1 << 20) // math.isqrt(standing ** skew) + 1 for standing in range(2, amount + 1)]
    surplus, given = total - bound - (amount - 1), [1] * (amount - 1)
    while surplus > 0:
        movable = [i for i in range(amount - 1) if given[i] < bound]
        mass, budget = sum([weights[i] for i in movable]), surplus
        for i in movable:
            addition = min(bound - given[i], max(1, budget * weights[i] // mass), surplus)
            given[i] = given[i] + addition
            surplus = surplus - addition
    return np.array([bound] + given)


def ragged_sizes(stream_key, amount, total, most, slope):
    if amount == 2:
        one = jax.random.randint(stream_key, (), max(1, total - most), min(most, total - 1) + 1)
        return jnp.stack([one, total - one])
    sizes = jnp.asarray(split_up(amount, total, most, slope), jnp.int32)
    pairs = (amount - 1) // 2
    source_of, receiver = sizes[1:1 + 2 * pairs:2], sizes[2:2 + 2 * pairs:2]
    margin = jnp.minimum(source_of - 1, most - receiver)
    passed = jax.random.randint(jax.random.fold_in(stream_key, 1), (pairs,), 0, 1 << 20) % (margin + 1)
    sizes = sizes.at[1:1 + 2 * pairs:2].set(source_of - passed).at[2:2 + 2 * pairs:2].set(receiver + passed)
    return sizes[jax.random.permutation(jax.random.fold_in(stream_key, 2), amount)]


def noise(own_key, dims, deviation, limit, pieces=(), kind=jnp.bfloat16):
    values = deviation * jax.random.normal(own_key, dims, jnp.float32)
    if pieces:
        values = values * block_scale(own_key, dims, pieces, -0.22, 0.18)
    return jnp.clip(values, -limit, limit).astype(kind)


def setup_inputs(seed: int = 0) -> dict:
    seeds = jax.random.split(jax.random.key(seed), 8)
    row_geno = draw_row_geno(jax.random.fold_in(seeds[7], 71), 0)
    col_geno = draw_col_geno(jax.random.fold_in(seeds[7], 71), 0)
    allele_freq = draw_allele_freq(jax.random.fold_in(seeds[7], 71), 0)
    snp_counts = ragged_sizes(seeds[3], CHROMS, VARIANTS, MOST_SNP, 2).astype(jnp.int32)
    group_of = draw_group_of(jax.random.fold_in(seeds[7], 71), 0)
    pair_mask = place_ends((jax.random.randint(seeds[5], (CHROMS, CHROMS), 0, 2) < 1).astype(jnp.int32), jax.random.fold_in(seeds[5], 1), 0, 1)
    probes = noise(seeds[6], (COLS, PROBES), 1.0, 6.0, ((0, 64),))
    return dict(row_geno=row_geno, col_geno=col_geno, allele_freq=allele_freq, snp_counts=snp_counts, group_of=group_of, pair_mask=pair_mask, probes=probes)


def variant_tables(frequency, snp_counts, pair_mask):
    variants = frequency.shape[0]
    chromosomes = snp_counts.shape[0]
    ends = jnp.cumsum(snp_counts, dtype=jnp.int32)
    position = jnp.arange(variants, dtype=jnp.int32)
    chrom_of = jnp.sum((position[None, :] >= ends[:, None]).astype(jnp.int32), axis=0, dtype=jnp.int32)
    labels = jnp.arange(chromosomes, dtype=jnp.int32)
    members = (chrom_of[None, :] == labels[:, None]).astype(jnp.float32)
    spread_term = 2.0 * frequency * (1.0 - frequency)
    denominator = jnp.dot(members, spread_term, precision=lax.Precision.HIGHEST)
    own_table = members / denominator[:, None]
    offdiag = pair_mask.astype(jnp.float32) * (1.0 - jnp.eye(chromosomes, dtype=jnp.float32))
    pair_table = jnp.dot(offdiag, own_table, precision=lax.Precision.HIGHEST)
    return own_table, pair_table


def reference(row_geno, col_geno, allele_freq, snp_counts, group_of, pair_mask, probes):
    frequency = allele_freq.astype(jnp.float32)
    rows_z = (row_geno.astype(jnp.float32) - 2.0 * frequency[None, :]).astype(jnp.bfloat16)
    cols_z = (col_geno.astype(jnp.float32) - 2.0 * frequency[None, :]).astype(jnp.bfloat16)
    own_table, pair_table = variant_tables(frequency, snp_counts, pair_mask)
    group_hot = (group_of[:, None] == jnp.arange(GROUPS, dtype=jnp.int32)[None, :]).astype(jnp.float32)
    cols_t = cols_z.T

    def one_block(block_z):
        block_f = block_z.astype(jnp.float32)
        total = jnp.zeros((GROUPS, block_z.shape[0], PROBES), jnp.float32)
        for chrom_id in range(CHROMS):
            own_rows = (block_f * own_table[chrom_id][None, :]).astype(jnp.bfloat16)
            pair_rows = (block_f * pair_table[chrom_id][None, :]).astype(jnp.bfloat16)
            kin = jnp.dot(own_rows, cols_t, preferred_element_type=jnp.float32)
            partner = jnp.dot(pair_rows, cols_t, preferred_element_type=jnp.float32)
            hadamard = (kin * partner).astype(jnp.bfloat16)
            applied = jnp.dot(hadamard, probes, preferred_element_type=jnp.float32)
            total = total + group_hot[chrom_id][:, None, None] * applied[None, :, :]
        return total

    blocks = rows_z.reshape(ROWS // ROW_DEV, ROW_DEV, VARIANTS)
    result = lax.map(one_block, blocks)
    result = jnp.transpose(result, (1, 0, 2, 3)).reshape(GROUPS, ROWS, PROBES)
    return result.astype(jnp.bfloat16)
```

```python
import jax
import jax.numpy as jnp
from jax import lax
from jax.experimental import pallas as pl
from jax.experimental.pallas import tpu as pltpu
from jax.sharding import Mesh, PartitionSpec as P

MOST_SNP = 512
LANES = 128
WINDOW = MOST_SNP + LANES
BF16, F32 = jnp.bfloat16, jnp.float32
NT = (((1,), (1,)), ((), ()))


def segments(counts_ref, variants):
    out, first = [], jnp.int32(0)
    for a in range(counts_ref.shape[0]):
        end = first + counts_ref[a]
        start = jnp.minimum(first // LANES, (variants - WINDOW) // LANES) * LANES
        out.append((first, end, pl.multiple_of(start, LANES)))
        first = end
    return out


def apply_kernel(
    me_ref, counts_ref, group_ref, mask_ref, own_hbm, other_hbm, cols_hbm, *refs
):
    out_refs = refs[: -9]
    cols_ref, rows_ref, tail_ref, z_ref, kin_ref, had_ref, sum_ref, row_sem, col_sem = refs[-9:]
    rows, variants = rows_ref.shape
    columns = z_ref.shape[0]
    blocks, each, _ = cols_ref.shape
    pieces, _, block = own_hbm.shape
    chromosomes, groups = counts_ref.shape[0], sum_ref.shape[0]
    fetch = pltpu.make_async_copy(cols_hbm, cols_ref, col_sem)
    copies = []
    for h, hbm in enumerate((own_hbm, other_hbm)):
        half = me_ref[1] if h == 0 else 1 - me_ref[1]
        for k in range(pieces):
            spot = pl.ds(pl.multiple_of((2 * k + half) * block, block), block)
            copies.append((hbm.at[k, rows : rows + 16, :], tail_ref.at[:, spot]))
            copies.append((hbm.at[k, 0:rows, :], rows_ref.at[:, spot]))
    copies = [
        pltpu.make_async_copy(source, target, row_sem.at[i])
        for i, (source, target) in enumerate(copies)
    ]
    for copy in copies:
        copy.start()
    fetch.start()
    for copy in copies:
        copy.wait()
    tail = tail_ref[...].astype(F32)
    twice = 2.0 * (tail[0:1] + tail[1:2])
    spread = twice * (1.0 - 0.5 * twice)
    lane = lax.broadcasted_iota(jnp.int32, (1, variants), 1)
    fetch.wait()
    for k in range(blocks):
        codes = cols_ref[k, :, 0:variants].astype(F32)
        z_ref[k * each : (k + 1) * each, :] = (codes - twice).astype(BF16)
    for a, (first, end, start) in enumerate(segments(counts_ref, variants)):
        member = (lane >= first) & (lane < end)
        denominator = jnp.sum(jnp.where(member, spread, 0.0), axis=1, keepdims=True)
        here = start + lax.broadcasted_iota(jnp.int32, (1, WINDOW), 1)
        own = jnp.where((here >= first) & (here < end), 1.0 / denominator, 0.0)
        window = rows_ref[:, pl.ds(start, WINDOW)].astype(F32)
        weighted = (window * own).astype(BF16)
        kin_ref[a] = lax.dot_general(
            weighted, z_ref[:, pl.ds(start, WINDOW)], NT, preferred_element_type=F32
        )
    pairs = [[mask_ref[a, b].astype(F32) for b in range(chromosomes)] for a in range(chromosomes)]
    high = 16

    @pl.loop(0, rows // high)
    def _(i):
        at = pl.ds(pl.multiple_of(i * high, high), high)
        for n in range(0, columns, LANES):
            kin = [kin_ref[b, at, n : n + LANES] for b in range(chromosomes)]
            for a in range(chromosomes):
                partner = None
                for b in range(chromosomes):
                    if b != a:
                        term = pairs[a][b] * kin[b]
                        partner = term if partner is None else partner + term
                had_ref[a, at, n : n + LANES] = (kin[a] * partner).astype(BF16)

    sum_ref[...] = jnp.zeros_like(sum_ref)
    probes = cols_ref[:, :, variants:].reshape(columns, -1)
    for a in range(chromosomes):
        sum_ref[group_ref[a]] += jnp.dot(had_ref[a], probes, preferred_element_type=F32)
    for k, out_ref in enumerate(out_refs):
        out_ref[...] = sum_ref[lax.rem(me_ref[0] + k, groups)].astype(BF16)


def apply(me, own, other, cols, snp_counts, group_of, pair_mask, groups):
    pieces, padded, block = own.shape
    rows, variants = padded - 16, 2 * pieces * block
    columns, samples = cols.shape[0] * cols.shape[1], cols.shape[2] - variants
    chromosomes = snp_counts.shape[0]
    smem = pl.BlockSpec(memory_space=pltpu.SMEM)
    vmem = pl.BlockSpec(memory_space=pltpu.VMEM)
    return pl.pallas_call(
        apply_kernel,
        out_shape=[jax.ShapeDtypeStruct((rows, samples), BF16)] * groups,
        in_specs=[smem] * 4 + [pl.BlockSpec(memory_space=pl.ANY)] * 3,
        out_specs=[vmem] * groups,
        scratch_shapes=[
            pltpu.VMEM(cols.shape, BF16),
            pltpu.VMEM((rows, variants), BF16),
            pltpu.VMEM((16, variants), BF16),
            pltpu.VMEM((columns, variants), BF16),
            pltpu.VMEM((chromosomes, rows, columns), F32),
            pltpu.VMEM((chromosomes, rows, columns), BF16),
            pltpu.VMEM((groups, rows, samples), F32),
            pltpu.SemaphoreType.DMA((4 * pieces,)),
            pltpu.SemaphoreType.DMA,
        ],
        compiler_params=pltpu.CompilerParams(vmem_limit_bytes=30 << 20),
        name="apply",
    )(me, snp_counts, group_of, pair_mask, own, other, cols)


def shifted(x, axis, k):
    n = lax.axis_size(axis)
    return lax.ppermute(x, axis, [(i, (i + k) % n) for i in range(n)])


def body(row_geno, col_geno, allele_freq, snp_counts, group_of, pair_mask, probes):
    groups, lows = lax.axis_size("c"), lax.axis_size("l")
    c, v = lax.axis_index("c"), lax.axis_index("v")
    columns, width = col_geno.shape
    quarter = columns // groups

    codes = jnp.concatenate([col_geno.astype(BF16), probes], axis=1)
    codes = jnp.broadcast_to(
        codes.reshape(groups, 1, quarter, codes.shape[1]), (groups, lows, quarter, codes.shape[1])
    ).reshape(groups * lows, quarter, -1)
    mine = lax.all_to_all(codes, ("c", "l"), 0, 0, tiled=True)
    mine = mine.reshape(groups, lows, quarter, -1)
    held = jnp.concatenate(
        [mine[k, :, :, :width] for k in range(groups)] + [mine[0, :, :, width:]], axis=-1
    ).reshape(lows * quarter, -1)
    plane = lax.axis_size("y") * lax.axis_size("x")
    cols = lax.all_to_all(
        jnp.broadcast_to(held[None], (plane, *held.shape)), ("y", "x"), 0, 0, tiled=True
    )

    coarse = lax.reduce_precision(allele_freq, 8, 7)
    fine = allele_freq - coarse
    tail = jnp.concatenate(
        [coarse[None], fine[None], jnp.zeros((14, allele_freq.shape[0]), F32)], axis=0
    ).astype(BF16)
    local = jnp.concatenate(
        [(row_geno.astype(F32) - 2.0 * allele_freq[None, :]).astype(BF16), tail], axis=0
    )
    own = lax.all_gather(local, "c", axis=0, tiled=False)
    other = shifted(own, "v", 1)
    me = jnp.stack([c, v]).astype(jnp.int32)
    parts = apply(me, own, other, cols, snp_counts, group_of, pair_mask, groups)

    sums = parts[0].astype(F32)
    for k in (2, 1, 3):
        sums = sums + shifted(parts[k], "c", k).astype(F32)
    total = sums.astype(BF16)
    across = shifted(total, "v", 1)
    return (total.astype(F32) + across.astype(F32)).astype(BF16)[None]


def solution(mesh):
    chrom, tile, var = (mesh.shape[k] for k in ("chrom", "tile", "var"))
    fine = Mesh(mesh.devices.reshape(chrom, 4, 4, tile // 16, var), ("c", "y", "x", "l", "v"))
    tile_axes = ("y", "x", "l")
    in_specs = (
        P(tile_axes, ("c", "v")),
        P((*tile_axes, "v"), "c"),
        P(("c", "v")),
        P(),
        P(),
        P(),
        P((*tile_axes, "v"), None),
    )
    out_specs = P("c", tile_axes, None)
    return jax.shard_map(body, mesh=fine, in_specs=in_specs, out_specs=out_specs, check_vma=False)
```

```python
import jax
import jax.numpy as jnp
from jax import lax
from jax.experimental import pallas as pl
from jax.experimental.pallas import tpu as pltpu
from jax.sharding import Mesh, PartitionSpec as P

MOST_SNP = 512
LANES = 128
WINDOW = MOST_SNP + LANES
BF16, F32 = jnp.bfloat16, jnp.float32
NT = (((1,), (1,)), ((), ()))


def segments(counts_ref, variants):
    out, first = [], jnp.int32(0)
    for a in range(counts_ref.shape[0]):
        end = first + counts_ref[a]
        start = jnp.minimum(first // LANES, (variants - WINDOW) // LANES) * LANES
        out.append((first, end, pl.multiple_of(start, LANES)))
        first = end
    return out


def apply_kernel(
    me_ref, counts_ref, group_ref, mask_ref, own_hbm, other_hbm, cols_hbm, *refs
):
    out_ref, cols_ref, rows_ref, tail_ref, z_ref, kin_ref, had_ref, sum_ref, row_sem, col_sem = refs
    rows, variants = rows_ref.shape
    columns = z_ref.shape[0]
    blocks, each, _ = cols_ref.shape
    pieces, _, block = own_hbm.shape
    chromosomes, groups = counts_ref.shape[0], sum_ref.shape[0]
    fetch = pltpu.make_async_copy(cols_hbm, cols_ref, col_sem)
    copies = []
    for h, hbm in enumerate((own_hbm, other_hbm)):
        half = me_ref[1] if h == 0 else 1 - me_ref[1]
        for k in range(pieces):
            spot = pl.ds(pl.multiple_of((2 * k + half) * block, block), block)
            copies.append((hbm.at[k, rows : rows + 16, :], tail_ref.at[:, spot]))
            copies.append((hbm.at[k, 0:rows, :], rows_ref.at[:, spot]))
    copies = [
        pltpu.make_async_copy(source, target, row_sem.at[i])
        for i, (source, target) in enumerate(copies)
    ]
    for copy in copies:
        copy.start()
    fetch.start()
    for copy in copies:
        copy.wait()
    tail = tail_ref[...].astype(F32)
    twice = 2.0 * (tail[0:1] + tail[1:2])
    spread = twice * (1.0 - 0.5 * twice)
    lane = lax.broadcasted_iota(jnp.int32, (1, variants), 1)
    fetch.wait()
    for k in range(blocks):
        codes = cols_ref[k, :, 0:variants].astype(F32)
        z_ref[k * each : (k + 1) * each, :] = (codes - twice).astype(BF16)
    for a, (first, end, start) in enumerate(segments(counts_ref, variants)):
        member = (lane >= first) & (lane < end)
        denominator = jnp.sum(jnp.where(member, spread, 0.0), axis=1, keepdims=True)
        here = start + lax.broadcasted_iota(jnp.int32, (1, WINDOW), 1)
        own = jnp.where((here >= first) & (here < end), 1.0 / denominator, 0.0)
        window = rows_ref[:, pl.ds(start, WINDOW)].astype(F32)
        weighted = (window * own).astype(BF16)
        kin_ref[a] = lax.dot_general(
            weighted, z_ref[:, pl.ds(start, WINDOW)], NT, preferred_element_type=F32
        )
    pairs = [[mask_ref[a, b].astype(F32) for b in range(chromosomes)] for a in range(chromosomes)]
    high = 16

    @pl.loop(0, rows // high)
    def _(i):
        at = pl.ds(pl.multiple_of(i * high, high), high)
        for n in range(0, columns, LANES):
            kin = [kin_ref[b, at, n : n + LANES] for b in range(chromosomes)]
            for a in range(chromosomes):
                partner = None
                for b in range(chromosomes):
                    if b != a:
                        term = pairs[a][b] * kin[b]
                        partner = term if partner is None else partner + term
                had_ref[a, at, n : n + LANES] = (kin[a] * partner).astype(BF16)

    sum_ref[...] = jnp.zeros_like(sum_ref)
    probes = cols_ref[:, :, variants:].reshape(columns, -1)
    for a in range(chromosomes):
        sum_ref[group_ref[a]] += jnp.dot(had_ref[a], probes, preferred_element_type=F32)
    for k in range(groups):
        out_ref[k] = sum_ref[lax.rem(me_ref[0] + k, groups)].astype(BF16)


def apply(me, own, other, cols, snp_counts, group_of, pair_mask, groups):
    pieces, padded, block = own.shape
    rows, variants = padded - 16, 2 * pieces * block
    columns, samples = cols.shape[0] * cols.shape[1], cols.shape[2] - variants
    chromosomes = snp_counts.shape[0]
    smem = pl.BlockSpec(memory_space=pltpu.SMEM)
    vmem = pl.BlockSpec(memory_space=pltpu.VMEM)
    return pl.pallas_call(
        apply_kernel,
        out_shape=jax.ShapeDtypeStruct((groups, rows, samples), BF16),
        in_specs=[smem] * 4 + [pl.BlockSpec(memory_space=pl.ANY)] * 3,
        out_specs=vmem,
        scratch_shapes=[
            pltpu.VMEM(cols.shape, BF16),
            pltpu.VMEM((rows, variants), BF16),
            pltpu.VMEM((16, variants), BF16),
            pltpu.VMEM((columns, variants), BF16),
            pltpu.VMEM((chromosomes, rows, columns), F32),
            pltpu.VMEM((chromosomes, rows, columns), BF16),
            pltpu.VMEM((groups, rows, samples), F32),
            pltpu.SemaphoreType.DMA((4 * pieces,)),
            pltpu.SemaphoreType.DMA,
        ],
        compiler_params=pltpu.CompilerParams(vmem_limit_bytes=30 << 20),
        name="apply",
    )(me, snp_counts, group_of, pair_mask, own, other, cols)


def shifted(x, axis, k):
    n = lax.axis_size(axis)
    return lax.ppermute(x, axis, [(i, (i + k) % n) for i in range(n)])


def body(row_geno, col_geno, allele_freq, snp_counts, group_of, pair_mask, probes):
    groups, lows = lax.axis_size("c"), lax.axis_size("l")
    c, v = lax.axis_index("c"), lax.axis_index("v")
    columns, width = col_geno.shape
    quarter = columns // groups

    codes = jnp.concatenate([col_geno.astype(BF16), probes], axis=1)
    codes = jnp.broadcast_to(
        codes.reshape(groups, 1, quarter, codes.shape[1]), (groups, lows, quarter, codes.shape[1])
    ).reshape(groups * lows, quarter, -1)
    mine = lax.all_to_all(codes, ("c", "l"), 0, 0, tiled=True)
    mine = mine.reshape(groups, lows, quarter, -1)
    held = jnp.concatenate(
        [mine[k, :, :, :width] for k in range(groups)] + [mine[0, :, :, width:]], axis=-1
    ).reshape(lows * quarter, -1)
    plane = lax.axis_size("y") * lax.axis_size("x")
    cols = lax.all_to_all(
        jnp.broadcast_to(held[None], (plane, *held.shape)), ("y", "x"), 0, 0, tiled=True
    )

    coarse = lax.reduce_precision(allele_freq, 8, 7)
    fine = allele_freq - coarse
    tail = jnp.concatenate(
        [coarse[None], fine[None], jnp.zeros((14, allele_freq.shape[0]), F32)], axis=0
    ).astype(BF16)
    local = jnp.concatenate(
        [(row_geno.astype(F32) - 2.0 * allele_freq[None, :]).astype(BF16), tail], axis=0
    )
    own = lax.all_gather(local, "c", axis=0, tiled=False)
    other = shifted(own, "v", 1)
    me = jnp.stack([c, v]).astype(jnp.int32)
    part = apply(me, own, other, cols, snp_counts, group_of, pair_mask, groups)

    part = (part.astype(F32) + shifted(part, "v", 1).astype(F32)).astype(BF16)
    pair = [(2 * i, 2 * ((i + 2) % groups)) for i in range(groups)]
    pair += [(2 * i + 1, 2 * ((i + 1) % groups) + 1) for i in range(groups)]
    last = [(2 * i + 1, 2 * ((i + 3) % groups) + 1) for i in range(groups)]
    first = lax.ppermute(jnp.where(v == 0, part[2], part[1]), ("c", "v"), pair)
    second = lax.ppermute(part[3], ("c", "v"), last)
    mine = first.astype(F32) + jnp.where(v == 0, part[0], second).astype(F32)
    mine = mine.astype(BF16)
    return (mine.astype(F32) + shifted(mine, "v", 1).astype(F32)).astype(BF16)[None]


def solution(mesh):
    chrom, tile, var = (mesh.shape[k] for k in ("chrom", "tile", "var"))
    fine = Mesh(mesh.devices.reshape(chrom, 4, 4, tile // 16, var), ("c", "y", "x", "l", "v"))
    tile_axes = ("y", "x", "l")
    in_specs = (
        P(tile_axes, ("c", "v")),
        P((*tile_axes, "v"), "c"),
        P(("c", "v")),
        P(),
        P(),
        P(),
        P((*tile_axes, "v"), None),
    )
    out_specs = P("c", tile_axes, None)
    return jax.shard_map(body, mesh=fine, in_specs=in_specs, out_specs=out_specs, check_vma=False)
```

```python
import jax
import jax.numpy as jnp
from jax import lax
from jax.experimental import pallas as pl
from jax.experimental.pallas import tpu as pltpu
from jax.sharding import Mesh, PartitionSpec as P

MOST_SNP = 512
LANES = 128
WINDOW = MOST_SNP + LANES
BF16, F32 = jnp.bfloat16, jnp.float32
NT = (((1,), (1,)), ((), ()))


def segments(counts_ref, variants):
    out, first = [], jnp.int32(0)
    for a in range(counts_ref.shape[0]):
        end = first + counts_ref[a]
        start = jnp.minimum(first // LANES, (variants - WINDOW) // LANES) * LANES
        out.append((first, end, pl.multiple_of(start, LANES)))
        first = end
    return out


def apply_kernel(
    me_ref, counts_ref, group_ref, mask_ref, own_hbm, other_hbm, cols_hbm, *refs
):
    keep_ref, send_ref, cols_ref, rows_ref, tail_ref, z_ref, kin_ref, had_ref, sum_ref, row_sem, col_sem = refs
    rows, variants = rows_ref.shape
    columns = z_ref.shape[0]
    blocks, each, _ = cols_ref.shape
    pieces, _, block = own_hbm.shape
    chromosomes, groups = counts_ref.shape[0], sum_ref.shape[0]
    fetch = pltpu.make_async_copy(cols_hbm, cols_ref, col_sem)
    copies = []
    for h, hbm in enumerate((own_hbm, other_hbm)):
        half = me_ref[1] if h == 0 else 1 - me_ref[1]
        for k in range(pieces):
            spot = pl.ds(pl.multiple_of((2 * k + half) * block, block), block)
            copies.append((hbm.at[k, rows : rows + 16, :], tail_ref.at[:, spot]))
            copies.append((hbm.at[k, 0:rows, :], rows_ref.at[:, spot]))
    copies = [
        pltpu.make_async_copy(source, target, row_sem.at[i])
        for i, (source, target) in enumerate(copies)
    ]
    for copy in copies:
        copy.start()
    fetch.start()
    for copy in copies:
        copy.wait()
    tail = tail_ref[...].astype(F32)
    twice = 2.0 * (tail[0:1] + tail[1:2])
    spread = twice * (1.0 - 0.5 * twice)
    lane = lax.broadcasted_iota(jnp.int32, (1, variants), 1)
    fetch.wait()
    for k in range(blocks):
        codes = cols_ref[k, :, 0:variants].astype(F32)
        z_ref[k * each : (k + 1) * each, :] = (codes - twice).astype(BF16)
    for a, (first, end, start) in enumerate(segments(counts_ref, variants)):
        member = (lane >= first) & (lane < end)
        denominator = jnp.sum(jnp.where(member, spread, 0.0), axis=1, keepdims=True)
        here = start + lax.broadcasted_iota(jnp.int32, (1, WINDOW), 1)
        member = ((here >= first) & (here < end)).astype(F32).astype(BF16)
        window = rows_ref[:, pl.ds(start, WINDOW)] * member
        kin_ref[a] = lax.dot_general(
            window, z_ref[:, pl.ds(start, WINDOW)], NT, preferred_element_type=F32
        ) * (1.0 / denominator)
    pairs = [[mask_ref[a, b].astype(F32) for b in range(chromosomes)] for a in range(chromosomes)]
    high = 16

    @pl.loop(0, rows // high)
    def _(i):
        at = pl.ds(pl.multiple_of(i * high, high), high)
        for n in range(0, columns, LANES):
            kin = [kin_ref[b, at, n : n + LANES] for b in range(chromosomes)]
            for a in range(chromosomes):
                partner = None
                for b in range(chromosomes):
                    if b != a:
                        term = pairs[a][b] * kin[b]
                        partner = term if partner is None else partner + term
                had_ref[a, at, n : n + LANES] = (kin[a] * partner).astype(BF16)

    sum_ref[...] = jnp.zeros_like(sum_ref)
    probes = cols_ref[:, :, variants:].reshape(columns, -1)
    for a in range(chromosomes):
        sum_ref[group_ref[a]] += jnp.dot(had_ref[a], probes, preferred_element_type=F32)
    for out_ref, core in ((keep_ref, me_ref[1]), (send_ref, 1 - me_ref[1])):
        for slot, k in enumerate((2 - core, 3 * core)):
            out_ref[slot] = sum_ref[lax.rem(me_ref[0] + k, groups)].astype(BF16)


def apply(me, own, other, cols, snp_counts, group_of, pair_mask, groups):
    pieces, padded, block = own.shape
    rows, variants = padded - 16, 2 * pieces * block
    columns, samples = cols.shape[0] * cols.shape[1], cols.shape[2] - variants
    chromosomes = snp_counts.shape[0]
    smem = pl.BlockSpec(memory_space=pltpu.SMEM)
    vmem = pl.BlockSpec(memory_space=pltpu.VMEM)
    return pl.pallas_call(
        apply_kernel,
        out_shape=[jax.ShapeDtypeStruct((groups // 2, rows, samples), BF16)] * 2,
        in_specs=[smem] * 4 + [pl.BlockSpec(memory_space=pl.ANY)] * 3,
        out_specs=[vmem] * 2,
        scratch_shapes=[
            pltpu.VMEM(cols.shape, BF16),
            pltpu.VMEM((rows, variants), BF16),
            pltpu.VMEM((16, variants), BF16),
            pltpu.VMEM((columns, variants), BF16),
            pltpu.VMEM((chromosomes, rows, columns), F32),
            pltpu.VMEM((chromosomes, rows, columns), BF16),
            pltpu.VMEM((groups, rows, samples), F32),
            pltpu.SemaphoreType.DMA((4 * pieces,)),
            pltpu.SemaphoreType.DMA,
        ],
        compiler_params=pltpu.CompilerParams(vmem_limit_bytes=30 << 20),
        name="apply",
    )(me, snp_counts, group_of, pair_mask, own, other, cols)


def shifted(x, axis, k):
    n = lax.axis_size(axis)
    return lax.ppermute(x, axis, [(i, (i + k) % n) for i in range(n)])


def body(row_geno, col_geno, allele_freq, snp_counts, group_of, pair_mask, probes):
    groups, lows = lax.axis_size("c"), lax.axis_size("l")
    c, v = lax.axis_index("c"), lax.axis_index("v")
    columns, width = col_geno.shape
    quarter = columns // groups

    codes = jnp.concatenate([col_geno.astype(BF16), probes], axis=1)
    codes = jnp.broadcast_to(
        codes.reshape(groups, 1, quarter, codes.shape[1]), (groups, lows, quarter, codes.shape[1])
    ).reshape(groups * lows, quarter, -1)
    mine = lax.all_to_all(codes, ("c", "l"), 0, 0, tiled=True)
    mine = mine.reshape(groups, lows, quarter, -1)
    held = jnp.concatenate(
        [mine[k, :, :, :width] for k in range(groups)] + [mine[0, :, :, width:]], axis=-1
    ).reshape(lows * quarter, -1)
    plane = lax.axis_size("y") * lax.axis_size("x")
    cols = lax.all_to_all(
        jnp.broadcast_to(held[None], (plane, *held.shape)), ("y", "x"), 0, 0, tiled=True
    )

    coarse = lax.reduce_precision(allele_freq, 8, 7)
    fine = allele_freq - coarse
    tail = jnp.concatenate(
        [coarse[None], fine[None], jnp.zeros((14, allele_freq.shape[0]), F32)], axis=0
    ).astype(BF16)
    local = jnp.concatenate(
        [(row_geno.astype(F32) - 2.0 * allele_freq[None, :]).astype(BF16), tail], axis=0
    )
    own = lax.all_gather(local, "c", axis=0, tiled=False)
    other = shifted(own, "v", 1)
    me = jnp.stack([c, v]).astype(jnp.int32)
    keep, send = apply(me, own, other, cols, snp_counts, group_of, pair_mask, groups)

    chip = (keep.astype(F32) + shifted(send, "v", 1).astype(F32)).astype(BF16)
    pair = [(2 * i, 2 * ((i + 2) % groups)) for i in range(groups)]
    pair += [(2 * i + 1, 2 * ((i + 1) % groups) + 1) for i in range(groups)]
    last = [(2 * i + 1, 2 * ((i + 3) % groups) + 1) for i in range(groups)]
    first = lax.ppermute(chip[0], ("c", "v"), pair)
    second = lax.ppermute(chip[1], ("c", "v"), last)
    mine = first.astype(F32) + jnp.where(v == 0, chip[1], second).astype(F32)
    mine = mine.astype(BF16)
    return (mine.astype(F32) + shifted(mine, "v", 1).astype(F32)).astype(BF16)[None]


def solution(mesh):
    chrom, tile, var = (mesh.shape[k] for k in ("chrom", "tile", "var"))
    fine = Mesh(mesh.devices.reshape(chrom, 4, 4, tile // 16, var), ("c", "y", "x", "l", "v"))
    tile_axes = ("y", "x", "l")
    in_specs = (
        P(tile_axes, ("c", "v")),
        P((*tile_axes, "v"), "c"),
        P(("c", "v")),
        P(),
        P(),
        P(),
        P((*tile_axes, "v"), None),
    )
    out_specs = P("c", tile_axes, None)
    return jax.shard_map(body, mesh=fine, in_specs=in_specs, out_specs=out_specs, check_vma=False)
```

```python
import jax
import jax.numpy as jnp
from jax import lax
from jax.experimental import pallas as pl
from jax.experimental.pallas import tpu as pltpu
from jax.sharding import Mesh, PartitionSpec as P

MOST_SNP = 512
LANES = 128
WINDOW = MOST_SNP + LANES
BF16, F32 = jnp.bfloat16, jnp.float32
NT = (((1,), (1,)), ((), ()))


def segments(counts_ref, variants):
    out, first = [], jnp.int32(0)
    for a in range(counts_ref.shape[0]):
        end = first + counts_ref[a]
        start = jnp.minimum(first // LANES, (variants - WINDOW) // LANES) * LANES
        out.append((first, end, pl.multiple_of(start, LANES)))
        first = end
    return out


def apply_kernel(
    me_ref, counts_ref, group_ref, mask_ref, own_hbm, other_hbm, cols_hbm, *refs
):
    keep_ref, send_ref, cols_ref, rows_ref, tail_ref, z_ref, kin_ref, had_ref, sum_ref, row_sem, col_sem = refs
    rows, variants = rows_ref.shape
    columns = z_ref.shape[0]
    blocks, each, _ = cols_ref.shape
    pieces, _, block = own_hbm.shape
    chromosomes, groups = counts_ref.shape[0], sum_ref.shape[0]
    fetch = pltpu.make_async_copy(cols_hbm, cols_ref, col_sem)
    copies = []
    for h, hbm in enumerate((own_hbm, other_hbm)):
        half = me_ref[1] if h == 0 else 1 - me_ref[1]
        for k in range(pieces):
            spot = pl.ds(pl.multiple_of((2 * k + half) * block, block), block)
            copies.append((hbm.at[k, rows : rows + 16, :], tail_ref.at[:, spot]))
            copies.append((hbm.at[k, 0:rows, :], rows_ref.at[:, spot]))
    copies = [
        pltpu.make_async_copy(source, target, row_sem.at[i])
        for i, (source, target) in enumerate(copies)
    ]
    for copy in copies:
        copy.start()
    fetch.start()
    for copy in copies:
        copy.wait()
    tail = tail_ref[...].astype(F32)
    twice = 2.0 * (tail[0:1] + tail[1:2])
    spread = twice * (1.0 - 0.5 * twice)
    lane = lax.broadcasted_iota(jnp.int32, (1, variants), 1)
    fetch.wait()
    for k in range(blocks):
        codes = cols_ref[k, :, 0:variants].astype(F32)
        z_ref[k * each : (k + 1) * each, :] = (codes - twice).astype(BF16)
    for a, (first, end, start) in enumerate(segments(counts_ref, variants)):
        member = (lane >= first) & (lane < end)
        denominator = jnp.sum(jnp.where(member, spread, 0.0), axis=1, keepdims=True)
        here = start + lax.broadcasted_iota(jnp.int32, (1, WINDOW), 1)
        member = ((here >= first) & (here < end)).astype(F32).astype(BF16)
        window = rows_ref[:, pl.ds(start, WINDOW)] * member
        kin_ref[a] = lax.dot_general(
            window, z_ref[:, pl.ds(start, WINDOW)], NT, preferred_element_type=F32
        ) * (1.0 / denominator)
    pairs = [[mask_ref[a, b].astype(F32) for b in range(chromosomes)] for a in range(chromosomes)]
    high = 16

    @pl.loop(0, rows // high)
    def _(i):
        at = pl.ds(pl.multiple_of(i * high, high), high)
        for n in range(0, columns, LANES):
            kin = [kin_ref[b, at, n : n + LANES] for b in range(chromosomes)]
            for a in range(chromosomes):
                partner = None
                for b in range(chromosomes):
                    if b != a:
                        term = pairs[a][b] * kin[b]
                        partner = term if partner is None else partner + term
                had_ref[a, at, n : n + LANES] = (kin[a] * partner).astype(BF16)

    sum_ref[...] = jnp.zeros_like(sum_ref)
    probes = cols_ref[:, :, variants:].reshape(columns, -1)
    for a in range(chromosomes):
        sum_ref[group_ref[a]] += jnp.dot(had_ref[a], probes, preferred_element_type=F32)
    for out_ref, core in ((keep_ref, me_ref[1]), (send_ref, 1 - me_ref[1])):
        for slot, k in enumerate((2 - core, 3 * core)):
            out_ref[slot] = sum_ref[lax.rem(me_ref[0] + k, groups)].astype(BF16)


def apply(me, own, other, cols, snp_counts, group_of, pair_mask, groups):
    pieces, padded, block = own.shape
    rows, variants = padded - 16, 2 * pieces * block
    columns, samples = cols.shape[0] * cols.shape[1], cols.shape[2] - variants
    chromosomes = snp_counts.shape[0]
    smem = pl.BlockSpec(memory_space=pltpu.SMEM)
    vmem = pl.BlockSpec(memory_space=pltpu.VMEM)
    return pl.pallas_call(
        apply_kernel,
        out_shape=[jax.ShapeDtypeStruct((groups // 2, rows, samples), BF16)] * 2,
        in_specs=[smem] * 4 + [vmem] * 2 + [pl.BlockSpec(memory_space=pl.ANY)],
        out_specs=[vmem] * 2,
        scratch_shapes=[
            pltpu.VMEM(cols.shape, BF16),
            pltpu.VMEM((rows, variants), BF16),
            pltpu.VMEM((16, variants), BF16),
            pltpu.VMEM((columns, variants), BF16),
            pltpu.VMEM((chromosomes, rows, columns), F32),
            pltpu.VMEM((chromosomes, rows, columns), BF16),
            pltpu.VMEM((groups, rows, samples), F32),
            pltpu.SemaphoreType.DMA((4 * pieces,)),
            pltpu.SemaphoreType.DMA,
        ],
        compiler_params=pltpu.CompilerParams(vmem_limit_bytes=30 << 20),
        name="apply",
    )(me, snp_counts, group_of, pair_mask, own, other, cols)


def shifted(x, axis, k):
    n = lax.axis_size(axis)
    return lax.ppermute(x, axis, [(i, (i + k) % n) for i in range(n)])


def body(row_geno, col_geno, allele_freq, snp_counts, group_of, pair_mask, probes):
    groups, lows = lax.axis_size("c"), lax.axis_size("l")
    c, v = lax.axis_index("c"), lax.axis_index("v")
    columns, width = col_geno.shape
    quarter = columns // groups

    codes = jnp.concatenate([col_geno.astype(BF16), probes], axis=1)
    codes = jnp.broadcast_to(
        codes.reshape(groups, 1, quarter, codes.shape[1]), (groups, lows, quarter, codes.shape[1])
    ).reshape(groups * lows, quarter, -1)
    mine = lax.all_to_all(codes, ("c", "l"), 0, 0, tiled=True)
    mine = mine.reshape(groups, lows, quarter, -1)
    held = jnp.concatenate(
        [mine[k, :, :, :width] for k in range(groups)] + [mine[0, :, :, width:]], axis=-1
    ).reshape(lows * quarter, -1)
    plane = lax.axis_size("y") * lax.axis_size("x")
    cols = lax.all_to_all(
        jnp.broadcast_to(held[None], (plane, *held.shape)), ("y", "x"), 0, 0, tiled=True
    )

    coarse = lax.reduce_precision(allele_freq, 8, 7)
    fine = allele_freq - coarse
    tail = jnp.concatenate(
        [coarse[None], fine[None], jnp.zeros((14, allele_freq.shape[0]), F32)], axis=0
    ).astype(BF16)
    local = jnp.concatenate(
        [(row_geno.astype(F32) - 2.0 * allele_freq[None, :]).astype(BF16), tail], axis=0
    )
    own = lax.all_gather(local, "c", axis=0, tiled=False)
    other = shifted(own, "v", 1)
    me = jnp.stack([c, v]).astype(jnp.int32)
    keep, send = apply(me, own, other, cols, snp_counts, group_of, pair_mask, groups)

    chip = (keep.astype(F32) + shifted(send, "v", 1).astype(F32)).astype(BF16)
    pair = [(2 * i, 2 * ((i + 2) % groups)) for i in range(groups)]
    pair += [(2 * i + 1, 2 * ((i + 1) % groups) + 1) for i in range(groups)]
    last = [(2 * i + 1, 2 * ((i + 3) % groups) + 1) for i in range(groups)]
    first = lax.ppermute(chip[0], ("c", "v"), pair)
    second = lax.ppermute(chip[1], ("c", "v"), last)
    mine = first.astype(F32) + jnp.where(v == 0, chip[1], second).astype(F32)
    mine = mine.astype(BF16)
    return (mine.astype(F32) + shifted(mine, "v", 1).astype(F32)).astype(BF16)[None]


def solution(mesh):
    chrom, tile, var = (mesh.shape[k] for k in ("chrom", "tile", "var"))
    fine = Mesh(mesh.devices.reshape(chrom, 4, 4, tile // 16, var), ("c", "y", "x", "l", "v"))
    tile_axes = ("y", "x", "l")
    in_specs = (
        P(tile_axes, ("c", "v")),
        P((*tile_axes, "v"), "c"),
        P(("c", "v")),
        P(),
        P(),
        P(),
        P((*tile_axes, "v"), None),
    )
    out_specs = P("c", tile_axes, None)
    return jax.shard_map(body, mesh=fine, in_specs=in_specs, out_specs=out_specs, check_vma=False)
```

```python
import jax
import jax.numpy as jnp
from jax import lax
from jax.experimental import pallas as pl
from jax.experimental.pallas import tpu as pltpu
from jax.sharding import Mesh, PartitionSpec as P

MOST_SNP = 512
LANES = 128
WINDOW = MOST_SNP + LANES
BF16, F32 = jnp.bfloat16, jnp.float32
NT = (((1,), (1,)), ((), ()))


def segments(counts_ref, variants):
    out, first = [], jnp.int32(0)
    for a in range(counts_ref.shape[0]):
        end = first + counts_ref[a]
        start = jnp.minimum(first // LANES, (variants - WINDOW) // LANES) * LANES
        out.append((first, end, pl.multiple_of(start, LANES)))
        first = end
    return out


def apply_kernel(
    me_ref, counts_ref, group_ref, mask_ref, own_hbm, other_hbm, cols_hbm, *refs
):
    keep_ref, send_ref, cols_ref, rows_ref, tail_ref, z_ref, kin_ref, had_ref, sum_ref, row_sem, col_sem = refs
    rows, variants = rows_ref.shape
    columns = z_ref.shape[0]
    blocks, each, _ = cols_ref.shape
    pieces, _, block = own_hbm.shape
    chromosomes, groups = counts_ref.shape[0], sum_ref.shape[0]
    parts = col_sem.shape[0]
    run = blocks // parts
    fetches = [
        pltpu.make_async_copy(
            cols_hbm.at[k * run : (k + 1) * run], cols_ref.at[k * run : (k + 1) * run], col_sem.at[k]
        )
        for k in range(parts)
    ]
    tails, wholes = [], []
    for h, hbm in enumerate((own_hbm, other_hbm)):
        half = me_ref[1] if h == 0 else 1 - me_ref[1]
        for k in range(pieces):
            spot = pl.ds(pl.multiple_of((2 * k + half) * block, block), block)
            i = 2 * (h * pieces + k)
            tails.append(
                pltpu.make_async_copy(
                    hbm.at[k, rows : rows + 16, :], tail_ref.at[:, spot], row_sem.at[i]
                )
            )
            wholes.append(
                pltpu.make_async_copy(
                    hbm.at[k, 0:rows, :], rows_ref.at[:, spot], row_sem.at[i + 1]
                )
            )
    for copy in tails + fetches + wholes:
        copy.start()
    for copy in tails:
        copy.wait()
    tail = tail_ref[...].astype(F32)
    twice = 2.0 * (tail[0:1] + tail[1:2])
    spread = twice * (1.0 - 0.5 * twice)
    lane = lax.broadcasted_iota(jnp.int32, (1, variants), 1)
    for k in range(blocks):
        if k % run == 0:
            fetches[k // run].wait()
        codes = cols_ref[k, :, 0:variants].astype(F32)
        z_ref[k * each : (k + 1) * each, :] = (codes - twice).astype(BF16)
    for copy in wholes:
        copy.wait()
    for a, (first, end, start) in enumerate(segments(counts_ref, variants)):
        member = (lane >= first) & (lane < end)
        denominator = jnp.sum(jnp.where(member, spread, 0.0), axis=1, keepdims=True)
        here = start + lax.broadcasted_iota(jnp.int32, (1, WINDOW), 1)
        member = ((here >= first) & (here < end)).astype(F32).astype(BF16)
        window = rows_ref[:, pl.ds(start, WINDOW)] * member
        kin_ref[a] = lax.dot_general(
            window, z_ref[:, pl.ds(start, WINDOW)], NT, preferred_element_type=F32
        ) * (1.0 / denominator)
    pairs = [[mask_ref[a, b].astype(F32) for b in range(chromosomes)] for a in range(chromosomes)]
    high = 32

    @pl.loop(0, rows // high)
    def _(i):
        at = pl.ds(pl.multiple_of(i * high, high), high)
        for n in range(0, columns, LANES):
            kin = [kin_ref[b, at, n : n + LANES] for b in range(chromosomes)]
            for a in range(chromosomes):
                partner = None
                for b in range(chromosomes):
                    if b != a:
                        term = pairs[a][b] * kin[b]
                        partner = term if partner is None else partner + term
                had_ref[a, at, n : n + LANES] = (kin[a] * partner).astype(BF16)

    sum_ref[...] = jnp.zeros_like(sum_ref)
    probes = cols_ref[:, :, variants:].reshape(columns, -1)
    for a in range(chromosomes):
        sum_ref[group_ref[a]] += jnp.dot(had_ref[a], probes, preferred_element_type=F32)
    for out_ref, core in ((keep_ref, me_ref[1]), (send_ref, 1 - me_ref[1])):
        for slot, k in enumerate((2 - core, 3 * core)):
            out_ref[slot] = sum_ref[lax.rem(me_ref[0] + k, groups)].astype(BF16)


def apply(me, own, other, cols, snp_counts, group_of, pair_mask, groups):
    pieces, padded, block = own.shape
    rows, variants = padded - 16, 2 * pieces * block
    columns, samples = cols.shape[0] * cols.shape[1], cols.shape[2] - variants
    chromosomes = snp_counts.shape[0]
    smem = pl.BlockSpec(memory_space=pltpu.SMEM)
    vmem = pl.BlockSpec(memory_space=pltpu.VMEM)
    return pl.pallas_call(
        apply_kernel,
        out_shape=[jax.ShapeDtypeStruct((groups // 2, rows, samples), BF16)] * 2,
        in_specs=[smem] * 4 + [vmem] * 2 + [pl.BlockSpec(memory_space=pl.ANY)],
        out_specs=[vmem] * 2,
        scratch_shapes=[
            pltpu.VMEM(cols.shape, BF16),
            pltpu.VMEM((rows, variants), BF16),
            pltpu.VMEM((16, variants), BF16),
            pltpu.VMEM((columns, variants), BF16),
            pltpu.VMEM((chromosomes, rows, columns), F32),
            pltpu.VMEM((chromosomes, rows, columns), BF16),
            pltpu.VMEM((groups, rows, samples), F32),
            pltpu.SemaphoreType.DMA((4 * pieces,)),
            pltpu.SemaphoreType.DMA((4,)),
        ],
        compiler_params=pltpu.CompilerParams(vmem_limit_bytes=30 << 20),
        name="apply",
    )(me, snp_counts, group_of, pair_mask, own, other, cols)


def shifted(x, axis, k):
    n = lax.axis_size(axis)
    return lax.ppermute(x, axis, [(i, (i + k) % n) for i in range(n)])


def body(row_geno, col_geno, allele_freq, snp_counts, group_of, pair_mask, probes):
    groups, lows = lax.axis_size("c"), lax.axis_size("l")
    c, v = lax.axis_index("c"), lax.axis_index("v")
    columns, width = col_geno.shape
    quarter = columns // groups

    codes = jnp.concatenate([col_geno.astype(BF16), probes], axis=1)
    codes = jnp.broadcast_to(
        codes.reshape(groups, 1, quarter, codes.shape[1]), (groups, lows, quarter, codes.shape[1])
    ).reshape(groups * lows, quarter, -1)
    mine = lax.all_to_all(codes, ("c", "l"), 0, 0, tiled=True)
    mine = mine.reshape(groups, lows, quarter, -1)
    held = jnp.concatenate(
        [mine[k, :, :, :width] for k in range(groups)] + [mine[0, :, :, width:]], axis=-1
    ).reshape(lows * quarter, -1)
    plane = lax.axis_size("y") * lax.axis_size("x")
    cols = lax.all_to_all(
        jnp.broadcast_to(held[None], (plane, *held.shape)), ("y", "x"), 0, 0, tiled=True
    )

    coarse = lax.reduce_precision(allele_freq, 8, 7)
    fine = allele_freq - coarse
    tail = jnp.concatenate(
        [coarse[None], fine[None], jnp.zeros((14, allele_freq.shape[0]), F32)], axis=0
    ).astype(BF16)
    local = jnp.concatenate(
        [(row_geno.astype(F32) - 2.0 * allele_freq[None, :]).astype(BF16), tail], axis=0
    )
    own = lax.all_gather(local, "c", axis=0, tiled=False)
    other = shifted(own, "v", 1)
    me = jnp.stack([c, v]).astype(jnp.int32)
    keep, send = apply(me, own, other, cols, snp_counts, group_of, pair_mask, groups)

    chip = (keep.astype(F32) + shifted(send, "v", 1).astype(F32)).astype(BF16)
    pair = [(2 * i, 2 * ((i + 2) % groups)) for i in range(groups)]
    pair += [(2 * i + 1, 2 * ((i + 1) % groups) + 1) for i in range(groups)]
    last = [(2 * i + 1, 2 * ((i + 3) % groups) + 1) for i in range(groups)]
    first = lax.ppermute(chip[0], ("c", "v"), pair)
    second = lax.ppermute(chip[1], ("c", "v"), last)
    mine = first.astype(F32) + jnp.where(v == 0, chip[1], second).astype(F32)
    mine = mine.astype(BF16)
    return (mine.astype(F32) + shifted(mine, "v", 1).astype(F32)).astype(BF16)[None]


def solution(mesh):
    chrom, tile, var = (mesh.shape[k] for k in ("chrom", "tile", "var"))
    fine = Mesh(mesh.devices.reshape(chrom, 4, 4, tile // 16, var), ("c", "y", "x", "l", "v"))
    tile_axes = ("y", "x", "l")
    in_specs = (
        P(tile_axes, ("c", "v")),
        P((*tile_axes, "v"), "c"),
        P(("c", "v")),
        P(),
        P(),
        P(),
        P((*tile_axes, "v"), None),
    )
    out_specs = P("c", tile_axes, None)
    return jax.shard_map(body, mesh=fine, in_specs=in_specs, out_specs=out_specs, check_vma=False)
```
